32 devices in a mesh: groups: 2 (over y), rows: 4 (over z), sub: 4 (over x, core).
Axes of the slice: x: 2, y: 2, z: 4, core: 2. Of those that a mesh axis runs over, the one named last changes fastest.
Arguments:
- embeddings: bfloat16 [8192, 1024], P(('groups', 'rows', 'sub')), parts along dimension 0, may hold values from -4 to 4
- pivots: int32 [4, 256], P('groups'), parts along dimension 0, may hold values from 0 to 4095, as said below
Outputs:
- whitened: float32 [8192, 512], P(('groups', 'rows', 'sub')), parts along dimension 0
The draws below stay inside these ranges and needn't reach their ends.
There are 2 independent parts, one for each index of `groups`. The reference program is written for one: setup_inputs(seed, part) draws one part's arguments, and reference() takes and returns one part's arrays. A program takes and returns all parts, laid end to end along the dimension named above; each array names one. Nothing has to cross between parts.
Inputs may be any that keep to these rules, and one draw needn't show every extreme that they name: `pivots`: the 512 pivot indices are all different.
All inputs are finite; a program needn't handle non-finite values.
Results may differ from the reference program's by a relative error of at most 0.0003.
Values may be sent and summed in bfloat16 or wider, within the bound.
A program may use at most 64 MiB of HBM per device.

```python
import jax
import jax.numpy as jnp
from jax import lax

EMBED = 1024
BLOCK = 256
BLOCKS = 2
POINTS = 4096


cluster_count = 64


def draw_embeddings(key, part):
    key = jax.random.fold_in(key, 11)
    key_one, key_two, key_three = jax.random.split(key, 3)
    centers = jax.random.normal(key_one, (cluster_count, EMBED), jnp.float32)
    labels = jax.random.randint(key_two, (POINTS,), 0, cluster_count)
    jitter = jax.random.normal(key_three, (POINTS, EMBED), jnp.float32)
    values = 0.8 * centers[labels] + 0.6 * jitter
    return jnp.clip(values, -4.0, 4.0).astype(jnp.bfloat16)


def draw_pivots(key, part):
    key = jax.random.fold_in(key, 5)
    key_one, key_two = jax.random.split(key)
    wanted = BLOCKS * BLOCK
    middle = jax.random.permutation(key_one, POINTS - 2)[:wanted - 2] + 1
    chosen = jnp.concatenate([middle, jnp.array([0, POINTS - 1], jnp.int32)])
    shuffle = jax.random.permutation(key_two, wanted)
    return chosen[shuffle].reshape(BLOCKS, BLOCK).astype(jnp.int32)


def setup_inputs(seed: int = 0, part: int = 0) -> dict:
    keys = jax.random.split(jax.random.key(seed), 3)
    own_keys = jax.random.split(jax.random.fold_in(keys[2], part), 3)
    return {
        "embeddings": draw_embeddings(jax.random.fold_in(jax.random.fold_in(keys[2], part), 71), part),
        "pivots": draw_pivots(jax.random.fold_in(jax.random.fold_in(keys[2], part), 71), part),
    }


ridge_shift = 0.001

def squares(points):
    return jnp.sum(jnp.square(points.astype(jnp.float32)), axis=1)

def kernel_tile(points, point_sq, others, other_sq):
    products = jnp.dot(points.astype(jnp.float32), others.T.astype(jnp.float32), preferred_element_type=jnp.float32)
    return jnp.exp((2.0 * products - point_sq[:, None] - other_sq[None, :]) / EMBED)

def exact_dot(first_set, second_set):
    return jnp.dot(first_set.astype(jnp.float32), second_set.astype(jnp.float32), precision=lax.Precision.HIGHEST, preferred_element_type=jnp.float32)

def lower_inverse(matrix):
    cholesky_low = jnp.linalg.cholesky(matrix)
    identity = jnp.eye(matrix.shape[0], dtype=jnp.float32)
    return jax.scipy.linalg.solve_triangular(cholesky_low, identity, lower=True)

def reference(embeddings, pivots):
    point_total = embeddings.shape[0]
    norms = squares(embeddings)
    factor = jnp.zeros((point_total, 0), jnp.float32)
    for section in range(BLOCKS):
        indices = pivots[section].astype(jnp.int32)
        piv_rows = embeddings[indices]
        piv_sq = norms[indices]
        residual = kernel_tile(embeddings, norms, piv_rows, piv_sq)
        pivot_gram = kernel_tile(piv_rows, piv_sq, piv_rows, piv_sq)
        if section > 0:
            piv_factor = factor[indices]
            residual = residual - exact_dot(factor, piv_factor.T)
            pivot_gram = pivot_gram - exact_dot(piv_factor, piv_factor.T)
        inverse = lower_inverse(pivot_gram)
        factor = jnp.concatenate([factor, exact_dot(residual, inverse.T)], axis=1)
    gram_sum = exact_dot(factor.T, factor) / point_total + ridge_shift * jnp.eye(factor.shape[1], dtype=jnp.float32)
    return exact_dot(factor, lower_inverse(gram_sum).T)
```

```python
import jax
import jax.numpy as jnp
from jax import lax
from jax.sharding import PartitionSpec as P

ridge_shift = 0.001
EXACT = lax.Precision.HIGHEST


def squares(points):
    return jnp.sum(jnp.square(points.astype(jnp.float32)), axis=1)


def kernel_tile(points, point_sq, others, other_sq):
    products = lax.dot_general(
        points, others, (((1,), (1,)), ((), ())), preferred_element_type=jnp.float32
    )
    return jnp.exp((2.0 * products - point_sq[:, None] - other_sq[None, :]) / points.shape[1])


def lower_inverse(matrix):
    cholesky_low = jnp.linalg.cholesky(matrix)
    identity = jnp.eye(matrix.shape[0], dtype=jnp.float32)
    return jax.scipy.linalg.solve_triangular(cholesky_low, identity, lower=True)


def on_device(embeddings, pivots):
    local_count, width = embeddings.shape
    devices = lax.axis_size(("rows", "sub"))
    first_row = lax.axis_index(("rows", "sub")) * local_count
    spots = pivots.reshape(-1) - first_row
    chosen = (spots[:, None] == lax.iota(jnp.int32, local_count)[None, :]).astype(jnp.bfloat16)
    mine = jnp.dot(chosen, embeddings, preferred_element_type=jnp.float32).astype(jnp.bfloat16)
    piv_rows = lax.psum(mine, ("rows", "sub"))
    norms = squares(embeddings)
    piv_sq = squares(piv_rows)
    tile = kernel_tile(embeddings, norms, piv_rows, piv_sq)
    gram = lax.psum(
        lax.dot_general(tile, tile, (((0,), (0,)), ((), ())), precision=EXACT), ("rows", "sub")
    )
    pivot_gram = kernel_tile(piv_rows, piv_sq, piv_rows, piv_sq)
    mixed = gram / (local_count * devices) + ridge_shift * pivot_gram
    return lax.dot_general(
        tile, lower_inverse(mixed), (((1,), (1,)), ((), ())), precision=EXACT
    )


def solution(mesh):
    return jax.shard_map(
        on_device,
        mesh=mesh,
        in_specs=(P(("groups", "rows", "sub"), None), P("groups", None)),
        out_specs=P(("groups", "rows", "sub"), None),
        check_vma=False,
    )
```

```python
import functools

import jax
import jax.numpy as jnp
from jax import lax
from jax.experimental import pallas as pl
from jax.experimental.pallas import tpu as pltpu
from jax.sharding import PartitionSpec as P

ridge_shift = 0.001
EXACT = lax.Precision.HIGHEST
GROUP = 16
TILE = 128


def squares(points):
    return jnp.sum(jnp.square(points.astype(jnp.float32)), axis=1)


def kernel_tile(points, point_sq, others, other_sq):
    products = lax.dot_general(
        points, others, (((1,), (1,)), ((), ())), preferred_element_type=jnp.float32
    )
    return jnp.exp((2.0 * products - point_sq[:, None] - other_sq[None, :]) / points.shape[1])


def exact_dot(first, second, first_dim, second_dim):
    return lax.dot_general(
        first,
        second,
        (((first_dim,), (second_dim,)), ((), ())),
        precision=EXACT,
        preferred_element_type=jnp.float32,
    )


def tile_inverse(tile):
    lane = lax.broadcasted_iota(jnp.int32, (GROUP, TILE), 1)
    sub = lax.broadcasted_iota(jnp.int32, (GROUP, TILE), 0)
    count = TILE // GROUP
    groups = [tile[g * GROUP:(g + 1) * GROUP] for g in range(count)]
    wide = functools.partial(jnp.broadcast_to, shape=(GROUP, TILE))
    for g in range(count):
        start = g * GROUP
        rows = groups[g]
        cols = [wide(rows[:, start + j:start + j + 1]) for j in range(GROUP)]
        for j in range(GROUP):
            scale = lax.rsqrt(wide(cols[j][j:j + 1]))
            below = jnp.where(sub > j, cols[j] * scale, 0.0)
            for k in range(j + 1, GROUP):
                cols[k] = cols[k] - below * (wide(cols[k][j:j + 1]) * scale)
            row = jnp.where(lane == start + j, scale, wide(rows[j:j + 1]) * scale)
            rest = jnp.where((lane == start + j) & (sub > j), 0.0, rows)
            rows = jnp.where(sub == j, row, rest - below * row)
        rows = jnp.where((lane > start + sub) & (lane < start + GROUP), 0.0, rows)
        groups[g] = rows
        if g + 1 < count:
            change = exact_dot(rows, rows, 0, 0)
            inside = (lane >= start) & (lane < start + GROUP)
            for h in range(g + 1, count):
                groups[h] = jnp.where(inside, 0.0, groups[h]) - change[h * GROUP:(h + 1) * GROUP]
    whole = jnp.concatenate(groups, axis=0)
    row_id = lax.broadcasted_iota(jnp.int32, (TILE, TILE), 0)
    lane_id = lax.broadcasted_iota(jnp.int32, (TILE, TILE), 1)
    return jnp.where(lane_id <= row_id, whole, 0.0)


def inverse_kernel(a_ref, w_ref, work):
    size = a_ref.shape[0]
    work[...] = a_ref[...]
    row_block = lax.broadcasted_iota(jnp.int32, (size, size), 0) // TILE
    col_block = lax.broadcasted_iota(jnp.int32, (size, size), 1) // TILE
    panel_block = lax.broadcasted_iota(jnp.int32, (TILE, size), 1) // TILE

    def step(block, carry):
        start = pl.multiple_of(block * TILE, TILE)
        here = pl.ds(start, TILE)
        small = tile_inverse(work[here, here])
        work[here, :] = exact_dot(small, work[here, :], 1, 0)
        work[here, here] = small
        panel = work[here, :]
        change = exact_dot(jnp.where(panel_block > block, panel, 0.0), panel, 0, 0)
        fresh = (row_block > block) & (col_block == block)
        work[...] = jnp.where(fresh, 0.0, work[...]) - change
        return carry

    lax.fori_loop(0, size // TILE, step, 0)
    row_id = lax.broadcasted_iota(jnp.int32, (size, size), 0)
    col_id = lax.broadcasted_iota(jnp.int32, (size, size), 1)
    w_ref[...] = jnp.where(col_id <= row_id, work[...], 0.0)


def lower_inverse(matrix):
    return pl.pallas_call(
        inverse_kernel,
        out_shape=jax.ShapeDtypeStruct(matrix.shape, jnp.float32),
        in_specs=[pl.BlockSpec(memory_space=pltpu.VMEM)],
        out_specs=pl.BlockSpec(memory_space=pltpu.VMEM),
        scratch_shapes=[pltpu.VMEM(matrix.shape, jnp.float32)],
        compiler_params=pltpu.CompilerParams(vmem_limit_bytes=32 * 2**20),
        name="lower_inverse",
    )(matrix)


def sum_kernel(in_ref, out_ref, half, quarter, parts, total, send, recv):
    pieces, rows, width = in_ref.shape
    z = lax.axis_index("rows")
    spot = lax.axis_index("sub")
    x, core = spot // 2, spot % 2
    peers = [{"sub": x * 2 + 1 - core}, {"sub": (1 - x) * 2 + core}]
    peers += [{"rows": (z + o) % 4} for o in (1, 2, 3)]
    barrier = pltpu.get_barrier_semaphore()
    for peer in peers:
        pl.semaphore_signal(barrier, inc=1, device_id=peer, device_id_type=pl.DeviceIdType.MESH)
    pl.semaphore_wait(barrier, len(peers))

    n2, n4, n16 = rows // 2, rows // 4, rows // 16

    def cut(start, size):
        return pl.ds(pl.multiple_of(start, n16), size)

    half_at = core * n2
    quarter_at = half_at + x * n4
    mine_at = quarter_at + z * n16

    def move(p, slot, src, dst, peer):
        return pltpu.make_async_remote_copy(
            src_ref=src, dst_ref=dst, send_sem=send.at[p, slot], recv_sem=recv.at[p, slot],
            device_id=peers[peer], device_id_type=pl.DeviceIdType.MESH,
        )

    first, second, third, fourth, fifth, sixth = [], [], [], [], [], []
    for p in range(pieces):
        copy = move(p, 0, in_ref.at[p, cut((1 - core) * n2, n2)], half.at[p], 0)
        copy.start()
        first.append(copy)
    for p in range(pieces):
        first[p].wait_recv()
        half[p] = half[p] + in_ref[p, cut(half_at, n2)]
        copy = move(p, 1, half.at[p, cut((1 - x) * n4, n4)], quarter.at[p], 1)
        copy.start()
        second.append(copy)
    for p in range(pieces):
        second[p].wait_recv()
        quarter[p] = quarter[p] + half[p, cut(x * n4, n4)]
        copies = []
        for o in (1, 2, 3):
            copy = move(p, 1 + o, quarter.at[p, cut(((z + o) % 4) * n16, n16)], parts.at[p, o - 1], 1 + o)
            copy.start()
            copies.append(copy)
        third.append(copies)
    for p in range(pieces):
        value = quarter[p, cut(z * n16, n16)]
        for o in (1, 2, 3):
            third[p][o - 1].wait_recv()
            value = value + parts[p, o - 1]
        total[p, cut(mine_at, n16)] = value
        copies = []
        for o in (1, 2, 3):
            place = total.at[p, cut(mine_at, n16)]
            copy = move(p, 4 + o, place, place, 1 + o)
            copy.start()
            copies.append(copy)
        fourth.append(copies)
    for p in range(pieces):
        for copy in fourth[p]:
            copy.wait_recv()
        place = total.at[p, cut(quarter_at, n4)]
        copy = move(p, 8, place, place, 1)
        copy.start()
        fifth.append(copy)
    for p in range(pieces):
        fifth[p].wait_recv()
        place = total.at[p, cut(half_at, n2)]
        copy = move(p, 9, place, place, 0)
        copy.start()
        sixth.append(copy)
    for p in range(pieces):
        sixth[p].wait_recv()
        out_ref[p] = total[p]
    for p in range(pieces):
        for copy in [first[p], second[p], *third[p], *fourth[p], fifth[p], sixth[p]]:
            copy.wait_send()


def group_sum(array, collective_id):
    if lax.axis_size("rows") != 4 or lax.axis_size("sub") != 4:
        return lax.psum(array, ("rows", "sub"))
    pieces, rows, width = array.shape
    kind = array.dtype
    return pl.pallas_call(
        sum_kernel,
        out_shape=jax.ShapeDtypeStruct(array.shape, kind),
        in_specs=[pl.BlockSpec(memory_space=pltpu.VMEM)],
        out_specs=pl.BlockSpec(memory_space=pltpu.VMEM),
        scratch_shapes=[
            pltpu.VMEM((pieces, rows // 2, width), kind),
            pltpu.VMEM((pieces, rows // 4, width), kind),
            pltpu.VMEM((pieces, 3, rows // 16, width), kind),
            pltpu.VMEM(array.shape, kind),
            pltpu.SemaphoreType.DMA((pieces, 10)),
            pltpu.SemaphoreType.DMA((pieces, 10)),
        ],
        compiler_params=pltpu.CompilerParams(
            collective_id=collective_id, has_side_effects=True, vmem_limit_bytes=32 * 2**20
        ),
        name="group_sum_" + str(collective_id),
    )(array)


def on_device(embeddings, pivots):
    local_count, width = embeddings.shape
    devices = lax.axis_size(("rows", "sub"))
    first_row = lax.axis_index(("rows", "sub")) * local_count
    spots = pivots.reshape(-1) - first_row
    count = spots.shape[0]
    chosen = (spots[:, None] == lax.iota(jnp.int32, local_count)[None, :]).astype(jnp.bfloat16)
    pieces = 4
    step = width // pieces
    mine = jnp.stack([
        jnp.dot(chosen, embeddings[:, p * step:(p + 1) * step], preferred_element_type=jnp.float32)
        .astype(jnp.bfloat16) for p in range(pieces)
    ])
    got = group_sum(mine, 0)
    piv_rows = jnp.concatenate([got[p] for p in range(pieces)], axis=1)
    norms = squares(embeddings)
    piv_sq = squares(piv_rows)
    tile = kernel_tile(embeddings, norms, piv_rows, piv_sq)
    pivot_gram = kernel_tile(piv_rows, piv_sq, piv_rows, piv_sq)
    factor = exact_dot(tile, lower_inverse(pivot_gram), 1, 1)
    share = exact_dot(factor, factor, 0, 0)
    low = count // 2
    packed = jnp.stack([share[:low, :low], share[low:, :low], share[low:, low:]])
    packed = group_sum(packed, 1) / (local_count * devices)
    gram = jnp.block([[packed[0], packed[1].T], [packed[1], packed[2]]])
    gram = gram + ridge_shift * jnp.eye(count, dtype=jnp.float32)
    return exact_dot(factor, lower_inverse(gram), 1, 1)


def solution(mesh):
    return jax.shard_map(
        on_device,
        mesh=mesh,
        in_specs=(P(("groups", "rows", "sub"), None), P("groups", None)),
        out_specs=P(("groups", "rows", "sub"), None),
        check_vma=False,
    )
```

```python
import functools

import jax
import jax.numpy as jnp
from jax import lax
from jax.experimental import pallas as pl
from jax.experimental.pallas import tpu as pltpu
from jax.sharding import PartitionSpec as P

ridge_shift = 0.001
EXACT = lax.Precision.HIGHEST
GROUP = 16
TILE = 128


def squares(points):
    return jnp.sum(jnp.square(points.astype(jnp.float32)), axis=1)


def kernel_tile(points, point_sq, others, other_sq):
    products = lax.dot_general(
        points, others, (((1,), (1,)), ((), ())), preferred_element_type=jnp.float32
    )
    return jnp.exp((2.0 * products - point_sq[:, None] - other_sq[None, :]) / points.shape[1])


def exact_dot(first, second, first_dim, second_dim):
    return lax.dot_general(
        first,
        second,
        (((first_dim,), (second_dim,)), ((), ())),
        precision=EXACT,
        preferred_element_type=jnp.float32,
    )


def tile_inverse(tile):
    lane = lax.broadcasted_iota(jnp.int32, (GROUP, TILE), 1)
    sub = lax.broadcasted_iota(jnp.int32, (GROUP, TILE), 0)
    count = TILE // GROUP
    groups = [tile[g * GROUP:(g + 1) * GROUP] for g in range(count)]
    wide = functools.partial(jnp.broadcast_to, shape=(GROUP, TILE))
    for g in range(count):
        start = g * GROUP
        end = start + GROUP
        rows = groups[g]
        cols = [wide(rows[:, start + j:start + j + 1]) for j in range(GROUP)]
        for j in range(GROUP):
            scale = lax.rsqrt(wide(cols[j][j:j + 1]))
            over = scale * scale
            for k in range(j + 1, GROUP):
                cols[k] = cols[k] - (cols[j] * wide(cols[k][j:j + 1])) * over
            below = jnp.where(sub > j, cols[j] * scale, 0.0)
            row = jnp.where(lane == start + j, scale, wide(rows[j:j + 1]) * scale)
            rest = jnp.where((lane == start + j) & (sub > j), 0.0, rows)
            rows = jnp.where(sub == j, row, rest - below * row)
        rows = jnp.where((lane > start + sub) & (lane < end), 0.0, rows)
        groups[g] = rows
        inside = (lane >= start) & (lane < end)
        if g + 1 < count:
            change = exact_dot(rows[:, end:end + GROUP], rows, 0, 0)
            groups[g + 1] = jnp.where(inside, 0.0, groups[g + 1]) - change
        if g + 2 < count:
            change = exact_dot(rows[:, end + GROUP:], rows, 0, 0)
            for h in range(g + 2, count):
                at = (h - g - 2) * GROUP
                groups[h] = jnp.where(inside, 0.0, groups[h]) - change[at:at + GROUP]
    whole = jnp.concatenate(groups, axis=0)
    row_id = lax.broadcasted_iota(jnp.int32, (TILE, TILE), 0)
    lane_id = lax.broadcasted_iota(jnp.int32, (TILE, TILE), 1)
    return jnp.where(lane_id <= row_id, whole, 0.0)


def inverse_kernel(a_ref, w_ref, upper):
    size = a_ref.shape[0]
    count = size // TILE
    w_ref[...] = jnp.zeros_like(w_ref)

    def at(block):
        return slice(block * TILE, (block + 1) * TILE)

    for j in range(count):
        square = a_ref[at(j), at(j)]
        for k in range(j):
            square = square - exact_dot(upper[at(k), at(j)], upper[at(k), at(j)], 0, 0)
        small = tile_inverse(square)
        for i in range(j + 1, count):
            block = a_ref[at(j), at(i)]
            for k in range(j):
                block = block - exact_dot(upper[at(k), at(j)], upper[at(k), at(i)], 0, 0)
            upper[at(j), at(i)] = exact_dot(small, block, 1, 0)
        w_ref[at(j), at(j)] = small
        if j:
            known = slice(0, j * TILE)
            left = exact_dot(upper[known, at(j)], w_ref[known, known], 0, 0)
            w_ref[at(j), known] = -exact_dot(small, left, 1, 0)


def lower_inverse(matrix):
    return pl.pallas_call(
        inverse_kernel,
        out_shape=jax.ShapeDtypeStruct(matrix.shape, jnp.float32),
        in_specs=[pl.BlockSpec(memory_space=pltpu.VMEM)],
        out_specs=pl.BlockSpec(memory_space=pltpu.VMEM),
        scratch_shapes=[pltpu.VMEM(matrix.shape, jnp.float32)],
        compiler_params=pltpu.CompilerParams(vmem_limit_bytes=32 * 2**20),
        name="lower_inverse",
    )(matrix)


def sum_kernel(in_ref, out_ref, half, quarter, parts, total, send, recv):
    pieces, rows, width = in_ref.shape
    z = lax.axis_index("rows")
    spot = lax.axis_index("sub")
    x, core = spot // 2, spot % 2
    peers = [{"sub": x * 2 + 1 - core}, {"sub": (1 - x) * 2 + core}]
    peers += [{"rows": (z + o) % 4} for o in (1, 2, 3)]
    barrier = pltpu.get_barrier_semaphore()
    for peer in peers:
        pl.semaphore_signal(barrier, inc=1, device_id=peer, device_id_type=pl.DeviceIdType.MESH)
    pl.semaphore_wait(barrier, len(peers))

    n2, n4, n16 = rows // 2, rows // 4, rows // 16

    def cut(start, size):
        return pl.ds(pl.multiple_of(start, n16), size)

    half_at = core * n2
    quarter_at = half_at + x * n4
    mine_at = quarter_at + z * n16

    def move(p, slot, src, dst, peer):
        return pltpu.make_async_remote_copy(
            src_ref=src, dst_ref=dst, send_sem=send.at[p, slot], recv_sem=recv.at[p, slot],
            device_id=peers[peer], device_id_type=pl.DeviceIdType.MESH,
        )

    first, second, third, fourth, fifth, sixth = [], [], [], [], [], []
    for p in range(pieces):
        copy = move(p, 0, in_ref.at[p, cut((1 - core) * n2, n2)], half.at[p], 0)
        copy.start()
        first.append(copy)
    for p in range(pieces):
        first[p].wait_recv()
        half[p] = half[p] + in_ref[p, cut(half_at, n2)]
        copy = move(p, 1, half.at[p, cut((1 - x) * n4, n4)], quarter.at[p], 1)
        copy.start()
        second.append(copy)
    for p in range(pieces):
        second[p].wait_recv()
        quarter[p] = quarter[p] + half[p, cut(x * n4, n4)]
        copies = []
        for o in (1, 2, 3):
            copy = move(p, 1 + o, quarter.at[p, cut(((z + o) % 4) * n16, n16)], parts.at[p, o - 1], 1 + o)
            copy.start()
            copies.append(copy)
        third.append(copies)
    for p in range(pieces):
        value = quarter[p, cut(z * n16, n16)]
        for o in (1, 2, 3):
            third[p][o - 1].wait_recv()
            value = value + parts[p, o - 1]
        total[p, cut(mine_at, n16)] = value
        copies = []
        for o in (1, 2, 3):
            place = total.at[p, cut(mine_at, n16)]
            copy = move(p, 4 + o, place, place, 1 + o)
            copy.start()
            copies.append(copy)
        fourth.append(copies)
    for p in range(pieces):
        for copy in fourth[p]:
            copy.wait_recv()
        place = total.at[p, cut(quarter_at, n4)]
        copy = move(p, 8, place, place, 1)
        copy.start()
        fifth.append(copy)
    for p in range(pieces):
        fifth[p].wait_recv()
        place = total.at[p, cut(half_at, n2)]
        copy = move(p, 9, place, place, 0)
        copy.start()
        sixth.append(copy)
    for p in range(pieces):
        sixth[p].wait_recv()
        out_ref[p] = total[p]
    for p in range(pieces):
        for copy in [first[p], second[p], *third[p], *fourth[p], fifth[p], sixth[p]]:
            copy.wait_send()


def group_sum(array, collective_id):
    if lax.axis_size("rows") != 4 or lax.axis_size("sub") != 4:
        return lax.psum(array, ("rows", "sub"))
    pieces, rows, width = array.shape
    kind = array.dtype
    return pl.pallas_call(
        sum_kernel,
        out_shape=jax.ShapeDtypeStruct(array.shape, kind),
        in_specs=[pl.BlockSpec(memory_space=pltpu.VMEM)],
        out_specs=pl.BlockSpec(memory_space=pltpu.VMEM),
        scratch_shapes=[
            pltpu.VMEM((pieces, rows // 2, width), kind),
            pltpu.VMEM((pieces, rows // 4, width), kind),
            pltpu.VMEM((pieces, 3, rows // 16, width), kind),
            pltpu.VMEM(array.shape, kind),
            pltpu.SemaphoreType.DMA((pieces, 10)),
            pltpu.SemaphoreType.DMA((pieces, 10)),
        ],
        compiler_params=pltpu.CompilerParams(
            collective_id=collective_id, has_side_effects=True, vmem_limit_bytes=32 * 2**20
        ),
        name="group_sum_" + str(collective_id),
    )(array)


def on_device(embeddings, pivots):
    local_count, width = embeddings.shape
    devices = lax.axis_size(("rows", "sub"))
    first_row = lax.axis_index(("rows", "sub")) * local_count
    spots = pivots.reshape(-1) - first_row
    count = spots.shape[0]
    chosen = (spots[:, None] == lax.iota(jnp.int32, local_count)[None, :]).astype(jnp.bfloat16)
    pieces = 4
    step = width // pieces
    mine = jnp.stack([
        jnp.dot(chosen, embeddings[:, p * step:(p + 1) * step], preferred_element_type=jnp.float32)
        .astype(jnp.bfloat16) for p in range(pieces)
    ])
    got = group_sum(mine, 0)
    piv_rows = jnp.concatenate([got[p] for p in range(pieces)], axis=1)
    norms = squares(embeddings)
    piv_sq = squares(piv_rows)
    tile = kernel_tile(embeddings, norms, piv_rows, piv_sq)
    pivot_gram = kernel_tile(piv_rows, piv_sq, piv_rows, piv_sq)
    factor = exact_dot(tile, lower_inverse(pivot_gram), 1, 1)
    share = exact_dot(factor, factor, 0, 0)
    low = count // 2
    packed = jnp.stack([share[:low, :low], share[low:, :low], share[low:, low:]])
    packed = group_sum(packed, 1) / (local_count * devices)
    gram = jnp.block([[packed[0], packed[1].T], [packed[1], packed[2]]])
    gram = gram + ridge_shift * jnp.eye(count, dtype=jnp.float32)
    return exact_dot(factor, lower_inverse(gram), 1, 1)


def solution(mesh):
    return jax.shard_map(
        on_device,
        mesh=mesh,
        in_specs=(P(("groups", "rows", "sub"), None), P("groups", None)),
        out_specs=P(("groups", "rows", "sub"), None),
        check_vma=False,
    )
```

```python
import functools

import jax
import jax.numpy as jnp
from jax import lax
from jax.experimental import pallas as pl
from jax.experimental.pallas import tpu as pltpu
from jax.sharding import PartitionSpec as P

ridge_shift = 0.001
EXACT = lax.Precision.HIGHEST
GROUP = 16
TILE = 128
PIECES = 4


def squares(points):
    return jnp.sum(jnp.square(points.astype(jnp.float32)), axis=1)


def kernel_tile(points, point_sq, others, other_sq):
    products = lax.dot_general(
        points, others, (((1,), (1,)), ((), ())), preferred_element_type=jnp.float32
    )
    return jnp.exp((2.0 * products - point_sq[:, None] - other_sq[None, :]) / points.shape[1])


def exact_dot(first, second, first_dim, second_dim):
    return lax.dot_general(
        first,
        second,
        (((first_dim,), (second_dim,)), ((), ())),
        precision=EXACT,
        preferred_element_type=jnp.float32,
    )


def tile_inverse(tile):
    lane = lax.broadcasted_iota(jnp.int32, (GROUP, TILE), 1)
    sub = lax.broadcasted_iota(jnp.int32, (GROUP, TILE), 0)
    count = TILE // GROUP
    groups = [tile[g * GROUP:(g + 1) * GROUP] for g in range(count)]
    wide = functools.partial(jnp.broadcast_to, shape=(GROUP, TILE))
    for g in range(count):
        start = g * GROUP
        end = start + GROUP
        rows = groups[g]
        cols = [wide(rows[:, start + j:start + j + 1]) for j in range(GROUP)]
        for j in range(GROUP):
            scale = lax.rsqrt(wide(cols[j][j:j + 1]))
            over = scale * scale
            for k in range(j + 1, GROUP):
                cols[k] = cols[k] - (cols[j] * wide(cols[k][j:j + 1])) * over
            below = jnp.where(sub > j, cols[j] * scale, 0.0)
            row = jnp.where(lane == start + j, scale, wide(rows[j:j + 1]) * scale)
            rest = jnp.where((lane == start + j) & (sub > j), 0.0, rows)
            rows = jnp.where(sub == j, row, rest - below * row)
        rows = jnp.where((lane > start + sub) & (lane < end), 0.0, rows)
        groups[g] = rows
        inside = (lane >= start) & (lane < end)
        if g + 1 < count:
            change = exact_dot(rows[:, end:end + GROUP], rows, 0, 0)
            groups[g + 1] = jnp.where(inside, 0.0, groups[g + 1]) - change
        if g + 2 < count:
            change = exact_dot(rows[:, end + GROUP:], rows, 0, 0)
            for h in range(g + 2, count):
                at = (h - g - 2) * GROUP
                groups[h] = jnp.where(inside, 0.0, groups[h]) - change[at:at + GROUP]
    whole = jnp.concatenate(groups, axis=0)
    row_id = lax.broadcasted_iota(jnp.int32, (TILE, TILE), 0)
    lane_id = lax.broadcasted_iota(jnp.int32, (TILE, TILE), 1)
    return jnp.where(lane_id <= row_id, whole, 0.0)


def inverse_kernel(a_ref, w_ref, upper):
    size = a_ref.shape[0]
    count = size // TILE
    w_ref[...] = jnp.zeros_like(w_ref)

    def at(block):
        return slice(block * TILE, (block + 1) * TILE)

    for j in range(count):
        square = a_ref[at(j), at(j)]
        for k in range(j):
            square = square - exact_dot(upper[at(k), at(j)], upper[at(k), at(j)], 0, 0)
        small = tile_inverse(square)
        for i in range(j + 1, count):
            block = a_ref[at(j), at(i)]
            for k in range(j):
                block = block - exact_dot(upper[at(k), at(j)], upper[at(k), at(i)], 0, 0)
            upper[at(j), at(i)] = exact_dot(small, block, 1, 0)
        w_ref[at(j), at(j)] = small
        if j:
            known = slice(0, j * TILE)
            left = exact_dot(upper[known, at(j)], w_ref[known, known], 0, 0)
            w_ref[at(j), known] = -exact_dot(small, left, 1, 0)


def lower_inverse(matrix):
    return pl.pallas_call(
        inverse_kernel,
        out_shape=jax.ShapeDtypeStruct(matrix.shape, jnp.float32),
        in_specs=[pl.BlockSpec(memory_space=pltpu.VMEM)],
        out_specs=pl.BlockSpec(memory_space=pltpu.VMEM),
        scratch_shapes=[pltpu.VMEM(matrix.shape, jnp.float32)],
        compiler_params=pltpu.CompilerParams(vmem_limit_bytes=32 * 2**20),
        name="lower_inverse",
    )(matrix)


def pick_rows(spots_ref, points_ref, mine, piece):
    local_count = points_ref.shape[0]
    width = mine.shape[2]
    lane = lax.broadcasted_iota(jnp.int32, (spots_ref.shape[0], local_count), 1)
    chosen = jnp.where(spots_ref[...] == lane, 1.0, 0.0).astype(jnp.bfloat16)
    block = points_ref[:, piece * width:(piece + 1) * width]
    rows = jnp.dot(chosen, block, preferred_element_type=jnp.float32)
    mine[piece] = rows.astype(mine.dtype)


def pivot_kernel(spots_ref, points_ref, out_ref, norm_ref, mine, *scratch):
    def beside():
        values = points_ref[...].astype(jnp.float32)
        norm_ref[...] = jnp.sum(values * values, axis=1, keepdims=True)

    pick = functools.partial(pick_rows, spots_ref, points_ref, mine)
    sum_kernel(mine, out_ref, *scratch, before=pick, beside=beside)


def sum_kernel(in_ref, out_ref, half, quarter, parts, total, send, recv, before=None, beside=None):
    pieces, rows, width = in_ref.shape
    z = lax.axis_index("rows")
    spot = lax.axis_index("sub")
    x, core = spot // 2, spot % 2
    peers = [{"sub": x * 2 + 1 - core}, {"sub": (1 - x) * 2 + core}]
    peers += [{"rows": (z + o) % 4} for o in (1, 2, 3)]
    barrier = pltpu.get_barrier_semaphore()
    for peer in peers:
        pl.semaphore_signal(barrier, inc=1, device_id=peer, device_id_type=pl.DeviceIdType.MESH)
    if before:
        before(0)
    pl.semaphore_wait(barrier, len(peers))

    n2, n4, n16 = rows // 2, rows // 4, rows // 16

    def cut(start, size):
        return pl.ds(pl.multiple_of(start, n16), size)

    half_at = core * n2
    quarter_at = half_at + x * n4
    mine_at = quarter_at + z * n16

    def move(p, slot, src, dst, peer):
        return pltpu.make_async_remote_copy(
            src_ref=src, dst_ref=dst, send_sem=send.at[p, slot], recv_sem=recv.at[p, slot],
            device_id=peers[peer], device_id_type=pl.DeviceIdType.MESH,
        )

    first, second, third, fourth, fifth, sixth = [], [], [], [], [], []
    for p in range(pieces):
        if before and p:
            before(p)
        copy = move(p, 0, in_ref.at[p, cut((1 - core) * n2, n2)], half.at[p], 0)
        copy.start()
        first.append(copy)
    for p in range(pieces):
        first[p].wait_recv()
        half[p] = half[p] + in_ref[p, cut(half_at, n2)]
        copy = move(p, 1, half.at[p, cut((1 - x) * n4, n4)], quarter.at[p], 1)
        copy.start()
        second.append(copy)
    for p in range(pieces):
        second[p].wait_recv()
        quarter[p] = quarter[p] + half[p, cut(x * n4, n4)]
        copies = []
        for o in (1, 2, 3):
            copy = move(p, 1 + o, quarter.at[p, cut(((z + o) % 4) * n16, n16)], parts.at[p, o - 1], 1 + o)
            copy.start()
            copies.append(copy)
        third.append(copies)
    if beside:
        beside()
    for p in range(pieces):
        value = quarter[p, cut(z * n16, n16)]
        for o in (1, 2, 3):
            third[p][o - 1].wait_recv()
            value = value + parts[p, o - 1]
        total[p, cut(mine_at, n16)] = value
        copies = []
        for o in (1, 2, 3):
            place = total.at[p, cut(mine_at, n16)]
            copy = move(p, 4 + o, place, place, 1 + o)
            copy.start()
            copies.append(copy)
        fourth.append(copies)
    for p in range(pieces):
        for copy in fourth[p]:
            copy.wait_recv()
        place = total.at[p, cut(quarter_at, n4)]
        copy = move(p, 8, place, place, 1)
        copy.start()
        fifth.append(copy)
    for p in range(pieces):
        fifth[p].wait_recv()
        place = total.at[p, cut(half_at, n2)]
        copy = move(p, 9, place, place, 0)
        copy.start()
        sixth.append(copy)
    for p in range(pieces):
        sixth[p].wait_recv()
        out_ref[p] = total[p]
    for p in range(pieces):
        for copy in [first[p], second[p], *third[p], *fourth[p], fifth[p], sixth[p]]:
            copy.wait_send()


def sum_scratch(shape, kind):
    pieces, rows, width = shape
    return [
        pltpu.VMEM((pieces, rows // 2, width), kind),
        pltpu.VMEM((pieces, rows // 4, width), kind),
        pltpu.VMEM((pieces, 3, rows // 16, width), kind),
        pltpu.VMEM(shape, kind),
        pltpu.SemaphoreType.DMA((pieces, 10)),
        pltpu.SemaphoreType.DMA((pieces, 10)),
    ]


def sum_params(collective_id):
    return pltpu.CompilerParams(
        collective_id=collective_id, has_side_effects=True, vmem_limit_bytes=32 * 2**20
    )


def sixteen():
    return lax.axis_size("rows") == 4 and lax.axis_size("sub") == 4


def group_sum(array, collective_id):
    if not sixteen():
        return lax.psum(array, ("rows", "sub"))
    return pl.pallas_call(
        sum_kernel,
        out_shape=jax.ShapeDtypeStruct(array.shape, array.dtype),
        in_specs=[pl.BlockSpec(memory_space=pltpu.VMEM)],
        out_specs=pl.BlockSpec(memory_space=pltpu.VMEM),
        scratch_shapes=sum_scratch(array.shape, array.dtype),
        compiler_params=sum_params(collective_id),
        name="group_sum_" + str(collective_id),
    )(array)


def gather_pivots(spots, points, collective_id):
    local_count, width = points.shape
    count = spots.shape[0]
    if not sixteen():
        chosen = (spots[:, None] == lax.iota(jnp.int32, local_count)[None, :]).astype(points.dtype)
        mine = jnp.dot(chosen, points, preferred_element_type=jnp.float32).astype(points.dtype)
        return lax.psum(mine, ("rows", "sub")), squares(points)
    shape = (PIECES, count, width // PIECES)
    got, norms = pl.pallas_call(
        pivot_kernel,
        out_shape=[
            jax.ShapeDtypeStruct(shape, points.dtype),
            jax.ShapeDtypeStruct((local_count, 1), jnp.float32),
        ],
        in_specs=[pl.BlockSpec(memory_space=pltpu.VMEM)] * 2,
        out_specs=[pl.BlockSpec(memory_space=pltpu.VMEM)] * 2,
        scratch_shapes=[pltpu.VMEM(shape, points.dtype), *sum_scratch(shape, points.dtype)],
        compiler_params=sum_params(collective_id),
        name="gather_pivots",
    )(spots[:, None], points)
    return jnp.concatenate([got[p] for p in range(PIECES)], axis=1), norms[:, 0]


def on_device(embeddings, pivots):
    local_count, width = embeddings.shape
    devices = lax.axis_size(("rows", "sub"))
    first_row = lax.axis_index(("rows", "sub")) * local_count
    spots = pivots.reshape(-1) - first_row
    count = spots.shape[0]
    piv_rows, norms = gather_pivots(spots, embeddings, 0)
    piv_sq = squares(piv_rows)
    tile = kernel_tile(embeddings, norms, piv_rows, piv_sq)
    pivot_gram = kernel_tile(piv_rows, piv_sq, piv_rows, piv_sq)
    factor = exact_dot(tile, lower_inverse(pivot_gram), 1, 1)
    share = exact_dot(factor, factor, 0, 0)
    low = count // 2
    packed = jnp.stack([share[:low, :low], share[low:, :low], share[low:, low:]])
    packed = group_sum(packed, 1) / (local_count * devices)
    gram = jnp.block([[packed[0], packed[1].T], [packed[1], packed[2]]])
    gram = gram + ridge_shift * jnp.eye(count, dtype=jnp.float32)
    return exact_dot(factor, lower_inverse(gram), 1, 1)


def solution(mesh):
    return jax.shard_map(
        on_device,
        mesh=mesh,
        in_specs=(P(("groups", "rows", "sub"), None), P("groups", None)),
        out_specs=P(("groups", "rows", "sub"), None),
        check_vma=False,
    )
```

```python
import functools

import jax
import jax.numpy as jnp
from jax import lax
from jax.experimental import pallas as pl
from jax.experimental.pallas import tpu as pltpu
from jax.sharding import PartitionSpec as P

ridge_shift = 0.001
EXACT = lax.Precision.HIGHEST
GROUP = 16
TILE = 128
PIECES = 4


def squares(points):
    return jnp.sum(jnp.square(points.astype(jnp.float32)), axis=1)


def kernel_tile(points, point_sq, others, other_sq):
    products = lax.dot_general(
        points, others, (((1,), (1,)), ((), ())), preferred_element_type=jnp.float32
    )
    return jnp.exp((2.0 * products - point_sq[:, None] - other_sq[None, :]) / points.shape[1])


def exact_dot(first, second, first_dim, second_dim):
    return lax.dot_general(
        first,
        second,
        (((first_dim,), (second_dim,)), ((), ())),
        precision=EXACT,
        preferred_element_type=jnp.float32,
    )


def tile_inverse(tile):
    lane = lax.broadcasted_iota(jnp.int32, (GROUP, TILE), 1)
    sub = lax.broadcasted_iota(jnp.int32, (GROUP, TILE), 0)
    count = TILE // GROUP
    groups = [tile[g * GROUP:(g + 1) * GROUP] for g in range(count)]
    wide = functools.partial(jnp.broadcast_to, shape=(GROUP, TILE))
    for g in range(count):
        start = g * GROUP
        end = start + GROUP
        rows = groups[g]
        cols = [wide(rows[:, start + j:start + j + 1]) for j in range(GROUP)]
        for j in range(GROUP):
            scale = lax.rsqrt(wide(cols[j][j:j + 1]))
            over = scale * scale
            for k in range(j + 1, GROUP):
                cols[k] = cols[k] - (cols[j] * wide(cols[k][j:j + 1])) * over
            below = jnp.where(sub > j, cols[j] * scale, 0.0)
            row = jnp.where(lane == start + j, scale, wide(rows[j:j + 1]) * scale)
            rest = jnp.where((lane == start + j) & (sub > j), 0.0, rows)
            rows = jnp.where(sub == j, row, rest - below * row)
        rows = jnp.where((lane > start + sub) & (lane < end), 0.0, rows)
        groups[g] = rows
        inside = (lane >= start) & (lane < end)
        if g + 1 < count:
            change = exact_dot(rows[:, end:end + GROUP], rows, 0, 0)
            groups[g + 1] = jnp.where(inside, 0.0, groups[g + 1]) - change
        if g + 2 < count:
            change = exact_dot(rows[:, end + GROUP:], rows, 0, 0)
            for h in range(g + 2, count):
                at = (h - g - 2) * GROUP
                groups[h] = jnp.where(inside, 0.0, groups[h]) - change[at:at + GROUP]
    whole = jnp.concatenate(groups, axis=0)
    row_id = lax.broadcasted_iota(jnp.int32, (TILE, TILE), 0)
    lane_id = lax.broadcasted_iota(jnp.int32, (TILE, TILE), 1)
    return jnp.where(lane_id <= row_id, whole, 0.0)


def inverse_kernel(a_ref, w_ref, upper):
    size = a_ref.shape[0]
    count = size // TILE
    w_ref[...] = jnp.zeros_like(w_ref)

    def at(block):
        return slice(block * TILE, (block + 1) * TILE)

    for j in range(count):
        square = a_ref[at(j), at(j)]
        for k in range(j):
            square = square - exact_dot(upper[at(k), at(j)], upper[at(k), at(j)], 0, 0)
        small = tile_inverse(square)
        for i in range(j + 1, count):
            block = a_ref[at(j), at(i)]
            for k in range(j):
                block = block - exact_dot(upper[at(k), at(j)], upper[at(k), at(i)], 0, 0)
            upper[at(j), at(i)] = exact_dot(small, block, 1, 0)
        w_ref[at(j), at(j)] = small
        if j:
            known = slice(0, j * TILE)
            left = exact_dot(upper[known, at(j)], w_ref[known, known], 0, 0)
            w_ref[at(j), known] = -exact_dot(small, left, 1, 0)


def lower_inverse(matrix):
    return pl.pallas_call(
        inverse_kernel,
        out_shape=jax.ShapeDtypeStruct(matrix.shape, jnp.float32),
        in_specs=[pl.BlockSpec(memory_space=pltpu.VMEM)],
        out_specs=pl.BlockSpec(memory_space=pltpu.VMEM),
        scratch_shapes=[pltpu.VMEM(matrix.shape, jnp.float32)],
        compiler_params=pltpu.CompilerParams(vmem_limit_bytes=32 * 2**20),
        name="lower_inverse",
    )(matrix)


def pick_rows(spots_ref, points_ref, mine, piece):
    local_count = points_ref.shape[0]
    width = mine.shape[2]
    lane = lax.broadcasted_iota(jnp.int32, (spots_ref.shape[0], local_count), 1)
    chosen = jnp.where(spots_ref[...] == lane, 1.0, 0.0).astype(jnp.bfloat16)
    block = points_ref[:, piece * width:(piece + 1) * width]
    rows = jnp.dot(chosen, block, preferred_element_type=jnp.float32)
    mine[piece] = rows.astype(mine.dtype)


def pivot_kernel(spots_ref, points_ref, out_ref, norm_ref, mine, *scratch):
    def beside():
        values = points_ref[...].astype(jnp.float32)
        norm_ref[...] = jnp.sum(values * values, axis=1, keepdims=True)

    pick = functools.partial(pick_rows, spots_ref, points_ref, mine)
    sum_kernel(mine, out_ref, *scratch, before=pick, beside=beside)


def sum_kernel(in_ref, out_ref, half, quarter, parts, total, send, recv, before=None, beside=None):
    pieces, rows, width = in_ref.shape
    z = lax.axis_index("rows")
    spot = lax.axis_index("sub")
    x, core = spot // 2, spot % 2
    peers = [{"sub": x * 2 + 1 - core}, {"sub": (1 - x) * 2 + core}]
    peers += [{"rows": (z + o) % 4} for o in (1, 2, 3)]
    barrier = pltpu.get_barrier_semaphore()
    for peer in peers:
        pl.semaphore_signal(barrier, inc=1, device_id=peer, device_id_type=pl.DeviceIdType.MESH)
    if before:
        before(0)
    pl.semaphore_wait(barrier, len(peers))

    n2, n4, n16 = rows // 2, rows // 4, rows // 16

    def cut(start, size):
        return pl.ds(pl.multiple_of(start, n16), size)

    half_at = core * n2
    quarter_at = half_at + x * n4
    mine_at = quarter_at + z * n16

    def move(p, slot, src, dst, peer):
        return pltpu.make_async_remote_copy(
            src_ref=src, dst_ref=dst, send_sem=send.at[p, slot], recv_sem=recv.at[p, slot],
            device_id=peers[peer], device_id_type=pl.DeviceIdType.MESH,
        )

    first, second, third, fourth, fifth, sixth = [], [], [], [], [], []
    for p in range(pieces):
        if before and p:
            before(p)
        copy = move(p, 0, in_ref.at[p, cut((1 - core) * n2, n2)], half.at[p], 0)
        copy.start()
        first.append(copy)
    for p in range(pieces):
        first[p].wait_recv()
        half[p] = half[p] + in_ref[p, cut(half_at, n2)]
        copy = move(p, 1, half.at[p, cut((1 - x) * n4, n4)], quarter.at[p], 1)
        copy.start()
        second.append(copy)
    for p in range(pieces):
        second[p].wait_recv()
        quarter[p] = quarter[p] + half[p, cut(x * n4, n4)]
        copies = []
        for o in (1, 2, 3):
            copy = move(p, 1 + o, quarter.at[p, cut(((z + o) % 4) * n16, n16)], parts.at[p, o - 1], 1 + o)
            copy.start()
            copies.append(copy)
        third.append(copies)
    if beside:
        beside()
    for p in range(pieces):
        value = quarter[p, cut(z * n16, n16)]
        for o in (1, 2, 3):
            third[p][o - 1].wait_recv()
            value = value + parts[p, o - 1]
        total[p, cut(mine_at, n16)] = value
        copies = []
        for o in (1, 2, 3):
            place = total.at[p, cut(mine_at, n16)]
            copy = move(p, 4 + o, place, place, 1 + o)
            copy.start()
            copies.append(copy)
        fourth.append(copies)
    for p in range(pieces):
        for copy in fourth[p]:
            copy.wait_recv()
        place = total.at[p, cut(quarter_at, n4)]
        copy = move(p, 8, place, place, 1)
        copy.start()
        fifth.append(copy)
    for p in range(pieces):
        fifth[p].wait_recv()
        place = total.at[p, cut(half_at, n2)]
        copy = move(p, 9, place, place, 0)
        copy.start()
        sixth.append(copy)
    for p in range(pieces):
        sixth[p].wait_recv()
        if before:
            out_ref[:, p * width:(p + 1) * width] = total[p]
        else:
            out_ref[p] = total[p]
    for p in range(pieces):
        for copy in [first[p], second[p], *third[p], *fourth[p], fifth[p], sixth[p]]:
            copy.wait_send()


def sum_scratch(shape, kind):
    pieces, rows, width = shape
    return [
        pltpu.VMEM((pieces, rows // 2, width), kind),
        pltpu.VMEM((pieces, rows // 4, width), kind),
        pltpu.VMEM((pieces, 3, rows // 16, width), kind),
        pltpu.VMEM(shape, kind),
        pltpu.SemaphoreType.DMA((pieces, 10)),
        pltpu.SemaphoreType.DMA((pieces, 10)),
    ]


def sum_params(collective_id):
    return pltpu.CompilerParams(
        collective_id=collective_id, has_side_effects=True, vmem_limit_bytes=32 * 2**20
    )


def sixteen():
    return lax.axis_size("rows") == 4 and lax.axis_size("sub") == 4


def group_sum(array, collective_id):
    if not sixteen():
        return lax.psum(array, ("rows", "sub"))
    return pl.pallas_call(
        sum_kernel,
        out_shape=jax.ShapeDtypeStruct(array.shape, array.dtype),
        in_specs=[pl.BlockSpec(memory_space=pltpu.VMEM)],
        out_specs=pl.BlockSpec(memory_space=pltpu.VMEM),
        scratch_shapes=sum_scratch(array.shape, array.dtype),
        compiler_params=sum_params(collective_id),
        name="group_sum_" + str(collective_id),
    )(array)


def gather_pivots(spots, points, collective_id):
    local_count, width = points.shape
    count = spots.shape[0]
    if not sixteen():
        chosen = (spots[:, None] == lax.iota(jnp.int32, local_count)[None, :]).astype(points.dtype)
        mine = jnp.dot(chosen, points, preferred_element_type=jnp.float32).astype(points.dtype)
        return lax.psum(mine, ("rows", "sub")), squares(points)
    shape = (PIECES, count, width // PIECES)
    got, norms = pl.pallas_call(
        pivot_kernel,
        out_shape=[
            jax.ShapeDtypeStruct((count, width), points.dtype),
            jax.ShapeDtypeStruct((local_count, 1), jnp.float32),
        ],
        in_specs=[pl.BlockSpec(memory_space=pltpu.VMEM)] * 2,
        out_specs=[pl.BlockSpec(memory_space=pltpu.VMEM)] * 2,
        scratch_shapes=[pltpu.VMEM(shape, points.dtype), *sum_scratch(shape, points.dtype)],
        compiler_params=sum_params(collective_id),
        name="gather_pivots",
    )(spots[:, None], points)
    return got, norms[:, 0]


def on_device(embeddings, pivots):
    local_count, width = embeddings.shape
    devices = lax.axis_size(("rows", "sub"))
    first_row = lax.axis_index(("rows", "sub")) * local_count
    spots = pivots.reshape(-1) - first_row
    count = spots.shape[0]
    piv_rows, norms = gather_pivots(spots, embeddings, 0)
    piv_sq = squares(piv_rows)
    tile = kernel_tile(embeddings, norms, piv_rows, piv_sq)
    pivot_gram = kernel_tile(piv_rows, piv_sq, piv_rows, piv_sq)
    factor = exact_dot(tile, lower_inverse(pivot_gram), 1, 1)
    share = exact_dot(factor, factor, 0, 0)
    blocks = range(count // TILE)
    pairs = [(i, j) for i in blocks for j in blocks if i <= j]
    packed = jnp.concatenate([
        share[i * TILE:(i + 1) * TILE, j * TILE:(j + 1) * TILE] for i, j in pairs
    ]).reshape(-1, 2 * TILE, TILE)
    packed = group_sum(packed, 1).reshape(-1, TILE, TILE) / (local_count * devices)
    empty = jnp.zeros((TILE, TILE), jnp.float32)
    gram = jnp.block([
        [packed[pairs.index((i, j))] if i <= j else empty for j in blocks] for i in blocks
    ])
    gram = gram + ridge_shift * jnp.eye(count, dtype=jnp.float32)
    return exact_dot(factor, lower_inverse(gram), 1, 1)


def solution(mesh):
    return jax.shard_map(
        on_device,
        mesh=mesh,
        in_specs=(P(("groups", "rows", "sub"), None), P("groups", None)),
        out_specs=P(("groups", "rows", "sub"), None),
        check_vma=False,
    )
```

```python
import functools

import jax
import jax.numpy as jnp
from jax import lax
from jax.experimental import pallas as pl
from jax.experimental.pallas import tpu as pltpu
from jax.sharding import PartitionSpec as P

ridge_shift = 0.001
EXACT = lax.Precision.HIGHEST
GROUP = 16
TILE = 128
PIECES = 4


def squares(points):
    return jnp.sum(jnp.square(points.astype(jnp.float32)), axis=1)


def kernel_tile(points, point_sq, others, other_sq):
    products = lax.dot_general(
        points, others, (((1,), (1,)), ((), ())), preferred_element_type=jnp.float32
    )
    return jnp.exp((2.0 * products - point_sq[:, None] - other_sq[None, :]) / points.shape[1])


def exact_dot(first, second, first_dim, second_dim):
    return lax.dot_general(
        first,
        second,
        (((first_dim,), (second_dim,)), ((), ())),
        precision=EXACT,
        preferred_element_type=jnp.float32,
    )


def tile_inverse(tile):
    lane = lax.broadcasted_iota(jnp.int32, (GROUP, TILE), 1)
    sub = lax.broadcasted_iota(jnp.int32, (GROUP, TILE), 0)
    count = TILE // GROUP
    groups = [tile[g * GROUP:(g + 1) * GROUP] for g in range(count)]
    wide = functools.partial(jnp.broadcast_to, shape=(GROUP, TILE))
    for g in range(count):
        start = g * GROUP
        end = start + GROUP
        rows = groups[g]
        cols = [wide(rows[:, start + j:start + j + 1]) for j in range(GROUP)]
        for j in range(GROUP):
            scale = lax.rsqrt(wide(cols[j][j:j + 1]))
            over = scale * scale
            for k in range(j + 1, GROUP):
                cols[k] = cols[k] - (cols[j] * wide(cols[k][j:j + 1])) * over
            below = jnp.where(sub > j, cols[j] * scale, 0.0)
            row = jnp.where(lane == start + j, scale, wide(rows[j:j + 1]) * scale)
            rest = jnp.where((lane == start + j) & (sub > j), 0.0, rows)
            rows = jnp.where(sub == j, row, rest - below * row)
        rows = jnp.where((lane > start + sub) & (lane < end), 0.0, rows)
        groups[g] = rows
        inside = (lane >= start) & (lane < end)
        if g + 1 < count:
            change = exact_dot(rows[:, end:end + GROUP], rows, 0, 0)
            groups[g + 1] = jnp.where(inside, 0.0, groups[g + 1]) - change
        if g + 2 < count:
            change = exact_dot(rows[:, end + GROUP:], rows, 0, 0)
            for h in range(g + 2, count):
                at = (h - g - 2) * GROUP
                groups[h] = jnp.where(inside, 0.0, groups[h]) - change[at:at + GROUP]
    whole = jnp.concatenate(groups, axis=0)
    row_id = lax.broadcasted_iota(jnp.int32, (TILE, TILE), 0)
    lane_id = lax.broadcasted_iota(jnp.int32, (TILE, TILE), 1)
    return jnp.where(lane_id <= row_id, whole, 0.0)


def inverse_kernel(a_ref, w_ref, upper):
    size = a_ref.shape[0]
    count = size // TILE
    w_ref[...] = jnp.zeros_like(w_ref)

    def at(block):
        return slice(block * TILE, (block + 1) * TILE)

    for j in range(count):
        square = a_ref[at(j), at(j)]
        for k in range(j):
            square = square - exact_dot(upper[at(k), at(j)], upper[at(k), at(j)], 0, 0)
        small = tile_inverse(square)
        for i in range(j + 1, count):
            block = a_ref[at(j), at(i)]
            for k in range(j):
                block = block - exact_dot(upper[at(k), at(j)], upper[at(k), at(i)], 0, 0)
            upper[at(j), at(i)] = exact_dot(small, block, 1, 0)
        w_ref[at(j), at(j)] = small
        if j:
            known = slice(0, j * TILE)
            left = exact_dot(upper[known, at(j)], w_ref[known, known], 0, 0)
            w_ref[at(j), known] = -exact_dot(small, left, 1, 0)


def lower_inverse(matrix):
    return pl.pallas_call(
        inverse_kernel,
        out_shape=jax.ShapeDtypeStruct(matrix.shape, jnp.float32),
        in_specs=[pl.BlockSpec(memory_space=pltpu.VMEM)],
        out_specs=pl.BlockSpec(memory_space=pltpu.VMEM),
        scratch_shapes=[pltpu.VMEM(matrix.shape, jnp.float32)],
        compiler_params=pltpu.CompilerParams(vmem_limit_bytes=32 * 2**20),
        name="lower_inverse",
    )(matrix)


def pick_rows(spots_ref, points_ref, mine, piece):
    local_count = points_ref.shape[0]
    width = mine.shape[2]
    lane = lax.broadcasted_iota(jnp.int32, (spots_ref.shape[0], local_count), 1)
    chosen = jnp.where(spots_ref[...] == lane, 1.0, 0.0).astype(jnp.bfloat16)
    block = points_ref[:, piece * width:(piece + 1) * width]
    rows = jnp.dot(chosen, block, preferred_element_type=jnp.float32)
    mine[piece] = rows.astype(mine.dtype)


def pivot_kernel(spots_ref, points_ref, out_ref, norm_ref, mine, *scratch):
    def beside():
        values = points_ref[...].astype(jnp.float32)
        norm_ref[...] = jnp.sum(values * values, axis=1, keepdims=True)

    pick = functools.partial(pick_rows, spots_ref, points_ref, mine)
    sum_kernel(mine, out_ref, *scratch, before=pick, beside=beside)


def sum_kernel(in_ref, out_ref, half, quarter, parts, total, send, recv, before=None, beside=None):
    pieces, rows, width = in_ref.shape
    z = lax.axis_index("rows")
    spot = lax.axis_index("sub")
    x, core = spot // 2, spot % 2
    peers = [{"sub": x * 2 + 1 - core}, {"sub": (1 - x) * 2 + core}]
    peers += [{"rows": (z + o) % 4} for o in (1, 2, 3)]
    barrier = pltpu.get_barrier_semaphore()
    for peer in peers:
        pl.semaphore_signal(barrier, inc=1, device_id=peer, device_id_type=pl.DeviceIdType.MESH)
    if before:
        before(0)
    pl.semaphore_wait(barrier, len(peers))

    n2, n4, n16 = rows // 2, rows // 4, rows // 16

    def cut(start, size):
        return pl.ds(pl.multiple_of(start, n16), size)

    half_at = core * n2
    quarter_at = half_at + x * n4
    mine_at = quarter_at + z * n16

    def move(p, slot, src, dst, peer):
        return pltpu.make_async_remote_copy(
            src_ref=src, dst_ref=dst, send_sem=send.at[p, slot], recv_sem=recv.at[p, slot],
            device_id=peers[peer], device_id_type=pl.DeviceIdType.MESH,
        )

    first, second, third, fourth, fifth, sixth = [], [], [], [], [], []
    def stage_1(p):
        if before and p:
            before(p)
        copy = move(p, 0, in_ref.at[p, cut((1 - core) * n2, n2)], half.at[p], 0)
        copy.start()
        first.append(copy)

    def stage_2(p):
        first[p].wait_recv()
        half[p] = half[p] + in_ref[p, cut(half_at, n2)]
        copy = move(p, 1, half.at[p, cut((1 - x) * n4, n4)], quarter.at[p], 1)
        copy.start()
        second.append(copy)

    def stage_3(p):
        second[p].wait_recv()
        quarter[p] = quarter[p] + half[p, cut(x * n4, n4)]
        copies = []
        for o in (1, 2, 3):
            copy = move(p, 1 + o, quarter.at[p, cut(((z + o) % 4) * n16, n16)], parts.at[p, o - 1], 1 + o)
            copy.start()
            copies.append(copy)
        third.append(copies)

    def stage_4(p):
        value = quarter[p, cut(z * n16, n16)]
        for o in (1, 2, 3):
            third[p][o - 1].wait_recv()
            value = value + parts[p, o - 1]
        total[p, cut(mine_at, n16)] = value
        copies = []
        for o in (1, 2, 3):
            place = total.at[p, cut(mine_at, n16)]
            copy = move(p, 4 + o, place, place, 1 + o)
            copy.start()
            copies.append(copy)
        fourth.append(copies)

    def stage_5(p):
        for copy in fourth[p]:
            copy.wait_recv()
        place = total.at[p, cut(quarter_at, n4)]
        copy = move(p, 8, place, place, 1)
        copy.start()
        fifth.append(copy)

    def stage_6(p):
        fifth[p].wait_recv()
        place = total.at[p, cut(half_at, n2)]
        copy = move(p, 9, place, place, 0)
        copy.start()
        sixth.append(copy)

    def stage_7(p):
        sixth[p].wait_recv()
        if before:
            out_ref[:, p * width:(p + 1) * width] = total[p]
        else:
            out_ref[p] = total[p]

    stages = [stage_1, stage_2, stage_3, stage_4, stage_5, stage_6, stage_7]
    for tick in range(pieces + len(stages) - 1):
        for level in reversed(range(len(stages))):
            if 0 <= tick - level < pieces:
                stages[level](tick - level)
        if beside and tick == pieces - 1:
            beside()
    for p in range(pieces):
        for copy in [first[p], second[p], *third[p], *fourth[p], fifth[p], sixth[p]]:
            copy.wait_send()


def sum_scratch(shape, kind):
    pieces, rows, width = shape
    return [
        pltpu.VMEM((pieces, rows // 2, width), kind),
        pltpu.VMEM((pieces, rows // 4, width), kind),
        pltpu.VMEM((pieces, 3, rows // 16, width), kind),
        pltpu.VMEM(shape, kind),
        pltpu.SemaphoreType.DMA((pieces, 10)),
        pltpu.SemaphoreType.DMA((pieces, 10)),
    ]


def sum_params(collective_id):
    return pltpu.CompilerParams(
        collective_id=collective_id, has_side_effects=True, vmem_limit_bytes=32 * 2**20
    )


def sixteen():
    return lax.axis_size("rows") == 4 and lax.axis_size("sub") == 4


def group_sum(array, collective_id):
    if not sixteen():
        return lax.psum(array, ("rows", "sub"))
    return pl.pallas_call(
        sum_kernel,
        out_shape=jax.ShapeDtypeStruct(array.shape, array.dtype),
        in_specs=[pl.BlockSpec(memory_space=pltpu.VMEM)],
        out_specs=pl.BlockSpec(memory_space=pltpu.VMEM),
        scratch_shapes=sum_scratch(array.shape, array.dtype),
        compiler_params=sum_params(collective_id),
        name="group_sum_" + str(collective_id),
    )(array)


def gather_pivots(spots, points, collective_id):
    local_count, width = points.shape
    count = spots.shape[0]
    if not sixteen():
        chosen = (spots[:, None] == lax.iota(jnp.int32, local_count)[None, :]).astype(points.dtype)
        mine = jnp.dot(chosen, points, preferred_element_type=jnp.float32).astype(points.dtype)
        return lax.psum(mine, ("rows", "sub")), squares(points)
    shape = (PIECES, count, width // PIECES)
    got, norms = pl.pallas_call(
        pivot_kernel,
        out_shape=[
            jax.ShapeDtypeStruct((count, width), points.dtype),
            jax.ShapeDtypeStruct((local_count, 1), jnp.float32),
        ],
        in_specs=[pl.BlockSpec(memory_space=pltpu.VMEM)] * 2,
        out_specs=[pl.BlockSpec(memory_space=pltpu.VMEM)] * 2,
        scratch_shapes=[pltpu.VMEM(shape, points.dtype), *sum_scratch(shape, points.dtype)],
        compiler_params=sum_params(collective_id),
        name="gather_pivots",
    )(spots[:, None], points)
    return got, norms[:, 0]


def on_device(embeddings, pivots):
    local_count, width = embeddings.shape
    devices = lax.axis_size(("rows", "sub"))
    first_row = lax.axis_index(("rows", "sub")) * local_count
    spots = pivots.reshape(-1) - first_row
    count = spots.shape[0]
    piv_rows, norms = gather_pivots(spots, embeddings, 0)
    piv_sq = squares(piv_rows)
    tile = kernel_tile(embeddings, norms, piv_rows, piv_sq)
    pivot_gram = kernel_tile(piv_rows, piv_sq, piv_rows, piv_sq)
    factor = exact_dot(tile, lower_inverse(pivot_gram), 1, 1)
    share = exact_dot(factor, factor, 0, 0)
    blocks = range(count // TILE)
    pairs = [(i, j) for i in blocks for j in blocks if i <= j]
    packed = jnp.concatenate([
        share[i * TILE:(i + 1) * TILE, j * TILE:(j + 1) * TILE] for i, j in pairs
    ]).reshape(-1, 2 * TILE, TILE)
    packed = group_sum(packed, 1).reshape(-1, TILE, TILE) / (local_count * devices)
    empty = jnp.zeros((TILE, TILE), jnp.float32)
    gram = jnp.block([
        [packed[pairs.index((i, j))] if i <= j else empty for j in blocks] for i in blocks
    ])
    gram = gram + ridge_shift * jnp.eye(count, dtype=jnp.float32)
    return exact_dot(factor, lower_inverse(gram), 1, 1)


def solution(mesh):
    return jax.shard_map(
        on_device,
        mesh=mesh,
        in_specs=(P(("groups", "rows", "sub"), None), P("groups", None)),
        out_specs=P(("groups", "rows", "sub"), None),
        check_vma=False,
    )
```
